32 devices in a mesh: dp: 4 (over z), expert: 8 (over y, x, core).
Axes of the slice: x: 2, y: 2, z: 4, core: 2. Of those that a mesh axis runs over, the one named last changes fastest.
Arguments:
- tokens: bfloat16 [4096, 2048], P(('dp', 'expert')), may hold values from -6 to 6
- expert_ids: int32 [4096, 2], P(('dp', 'expert')), may hold values from 0 to 7, all different within a row; in each aligned block of 128 rows (0 to 127, 128 to 255, ...) at most 36 rows name the same one
- gate_levels: int32 [4096, 2], P(('dp', 'expert')), may hold values from 26 to 255
- inner_weight: bfloat16 [8, 2048, 4096], P('expert', None, 'dp'), may hold values from -0.125 to 0.125
- outer_weight: bfloat16 [8, 2048, 4096], P('expert', None, 'dp'), may hold values from -0.09375 to 0.09375
- pair_flags: int32 [8], P('expert'), may hold values from 0 to 1, as said below
Outputs:
- mixture: bfloat16 [4096, 2048], P(('dp', 'expert'))
- placed_inner: bfloat16 [8, 2048, 4096], P('expert', None, 'dp')
- placed_outer: bfloat16 [8, 2048, 4096], P('expert', None, 'dp')
The draws below stay inside these ranges and needn't reach their ends.
Inputs may be any that keep to these rules, and one draw needn't show every extreme that they name: `expert_ids`: among the rows of one device, no expert is named by more than 36 rows, a bound that some block reaches; the two experts of a row differ. pair_flags[e] equals pair_flags[(e + 4) mod 8]; some pair has 1 and some pair has 0.
All inputs are finite; a program needn't handle non-finite values.
Results may differ from the reference program's by a relative error of at most 0.0065.
Values may be sent and summed in bfloat16 or wider, within the bound.
No kernel may reach another device: no remote copies, remote signals or barrier semaphores. Data moves between devices by JAX's collectives and lax.ppermute only.
A program may use at most 128 MiB of HBM per device.

```python
import math
import jax
import jax.numpy as jnp
import numpy as np
from jax import lax

D = 2048
FF = 4096
TOK_DEV = 128
EXPERTS = 8
CAP = 36
TOKENS = 4096
N_DP = 4


def draw_pair_flags(key, part):
    half_way = EXPERTS // 2
    first_key = jax.random.fold_in(key, 11)
    second_key = jax.random.fold_in(key, 23)
    third_key = jax.random.fold_in(key, 37)
    halves = jax.random.randint(first_key, (half_way,), 0, 2, dtype=jnp.int32)
    chosen = jax.random.randint(second_key, (), 0, half_way, dtype=jnp.int32)
    step_on = jax.random.randint(third_key, (), 1, half_way, dtype=jnp.int32)
    other = ((chosen + step_on) % half_way).astype(jnp.int32)
    halves = halves.at[chosen].set(1)
    halves = halves.at[other].set(0)
    return jnp.concatenate([halves, halves]).astype(jnp.int32)


def touch_ends(array, rng, least, largest):
    longest = array.shape.index(max(array.shape))
    spots = []
    for shift in (0, 1):
        where = [jax.random.randint(jax.random.fold_in(rng, axis), (), 0, length) for axis, length in enumerate(array.shape)]
        where[longest] = (where[longest] + shift) % array.shape[longest]
        spots.append(tuple(where))
    return array.at[spots[0]].set(least).at[spots[1]].set(largest)


def block_scale(key, dims, shards, least, largest):
    loudness, own = 1.0, jax.random.fold_in(key, 6)
    for axis_at, shards_of in shards:
        draws = jnp.exp(jax.random.uniform(jax.random.fold_in(own, axis_at), (shards_of,), jnp.float32, least / len(shards), largest / len(shards)))
        loudness = loudness * jnp.repeat(draws, dims[axis_at] // shards_of).reshape([-1 if axis == axis_at else 1 for axis in range(len(dims))])
    return loudness


def deal_out(key, own, number, rows, amount, top, reach, skew):
    order = jax.random.permutation(key, amount)
    packed, ordinary = portions_of(amount, rows * top, reach, skew, True), portions_of(amount, rows * top, reach, skew, False)
    places = jnp.arange(amount)

    def named(sizes, offset_by):
        used = int((sizes > 0).sum())
        fixed = max(1, used // 4)
        moved = fixed + (places - fixed + offset_by * (used - fixed)) % max(1, amount - fixed)
        return jnp.zeros((amount,), jnp.int32).at[order[jnp.where(places < fixed, places, moved)]].set(jnp.asarray(sizes, jnp.int32))

    sizes = jnp.where(number % 4 == 0, named(packed, number // 4), named(ordinary, number - number // 4 - 1))
    mixed = jax.random.permutation(jax.random.fold_in(own, 3), amount)
    donor, taker = mixed[0:amount // 2 * 2:2], mixed[1:amount // 2 * 2:2]
    room = jnp.minimum(sizes[donor] - 1, reach - sizes[taker]) // 2
    room = jnp.where((donor == order[0]) | (taker == order[0]) | (sizes[taker] == 0), 0, jnp.maximum(room, 0))
    moved = jax.random.randint(jax.random.fold_in(own, 4), (amount // 2,), 0, 1 << 20) % (room + 1)
    sizes = sizes.at[donor].add(-moved).at[taker].add(moved)
    members = jnp.searchsorted(jnp.cumsum(sizes), jnp.arange(rows * top), side="right").astype(jnp.int32)
    listing = members.reshape(top, rows).T
    listing = listing[jax.random.permutation(jax.random.fold_in(own, 1), rows)]
    offset_by = jax.random.randint(jax.random.fold_in(own, 2), (rows, 1), 0, top)
    return jnp.take_along_axis(listing, (jnp.arange(top)[None, :] + offset_by) % top, axis=1)


def portions_of(count, total, reach, skew, full):
    weights = [(1 << 20) // math.isqrt(rank ** skew) + 1 for rank in range(1, count + 1)]
    largest = reach if full else min(reach, max(-(-total // count), total * weights[0] // sum(weights)))
    least = 1 if total - largest >= count - 1 else 0
    given, spare = [largest] + [least] * (count - 1), total - largest - least * (count - 1)
    while spare > 0:
        free = [i for i in range(1, count) if given[i] < largest] or [i for i in range(1, count) if given[i] < reach]
        pool, budget = sum([weights[i] for i in free]), spare
        for i in free:
            more = min(reach - given[i], max(1, budget * weights[i] // pool), spare)
            given[i] = given[i] + more
            spare = spare - more
    return np.array(given)


def scatter_about(stream_key, shape, deviation, reach, cuts=(), kind=jnp.bfloat16):
    result = jax.random.normal(stream_key, shape, jnp.float32) * deviation
    if len(cuts) > 0:
        result = block_scale(stream_key, shape, cuts, -0.22, 0.18) * result
    return jnp.clip(result, min=-reach, max=reach).astype(kind)


def setup_inputs(seed: int = 0) -> dict:
    seeds = jax.random.split(jax.random.key(seed), 7)
    tokens = scatter_about(seeds[0], (TOKENS, D), 1.0, 6.0, ((0, 32),))
    expert_ids_keys = jax.random.split(jax.random.fold_in(seeds[1], 1), TOKENS // TOK_DEV)
    expert_ids_turns = jax.random.permutation(jax.random.fold_in(seeds[1], 3), TOKENS // TOK_DEV)
    expert_ids = jax.vmap(lambda own, number: deal_out(jax.random.fold_in(seeds[1], 2), own, number, TOK_DEV, EXPERTS, 2, CAP, 2))(expert_ids_keys, expert_ids_turns).reshape((TOKENS, 2))
    gate_levels = touch_ends(jax.random.randint(seeds[2], (TOKENS, 2), 26, 256), jax.random.fold_in(seeds[2], 1), 26, 255).astype(jnp.int32)
    inner_weight = scatter_about(seeds[3], (EXPERTS, D, FF), D ** -0.5, 0.125, ((0, 8), (2, 4)))
    outer_weight = scatter_about(seeds[4], (EXPERTS, D, FF), FF ** -0.5, 0.09375, ((0, 8), (2, 4)))
    pair_flags = draw_pair_flags(jax.random.fold_in(seeds[6], 71), 0)
    return dict(tokens=tokens, expert_ids=expert_ids, gate_levels=gate_levels, inner_weight=inner_weight, outer_weight=outer_weight, pair_flags=pair_flags)


def reference(tokens, expert_ids, gate_levels, inner_weight, outer_weight, pair_flags):
    half_way = EXPERTS // 2
    partner = ((jnp.arange(EXPERTS, dtype=jnp.int32) + half_way) % EXPERTS).astype(jnp.int32)
    traded = (pair_flags == 1)[:, None, None]
    placed_inner = jnp.where(traded, inner_weight[partner], inner_weight)
    placed_outer = jnp.where(traded, outer_weight[partner], outer_weight)
    flat_ids = expert_ids.reshape(-1).astype(jnp.int32)
    order = jnp.argsort(flat_ids, stable=True).astype(jnp.int32)
    matches = (flat_ids[None, :] == jnp.arange(EXPERTS, dtype=jnp.int32)[:, None]).astype(jnp.int32)
    counts = jnp.sum(matches, axis=1).astype(jnp.int32)
    offsets = (jnp.cumsum(counts) - counts).astype(jnp.int32)
    most_rows = CAP * (TOKENS // TOK_DEV)
    padded = jnp.concatenate([(order // 2).astype(jnp.int32), jnp.zeros((most_rows,), jnp.int32)])
    gates = gate_levels.astype(jnp.float32) / 256.0
    slice_width = FF // N_DP
    total = jnp.zeros((TOKENS, D), jnp.float32)
    for slice_no in range(N_DP):
        low_col = slice_no * slice_width

        def per_expert(buffer, expert):
            start = offsets[expert]
            picked = lax.dynamic_slice_in_dim(padded, start, most_rows)
            rows = tokens[picked].astype(jnp.float32)
            inner = lax.dynamic_index_in_dim(inner_weight, expert, 0, keepdims=False)
            outer = lax.dynamic_index_in_dim(outer_weight, expert, 0, keepdims=False)
            inner = inner[:, low_col:low_col + slice_width].astype(jnp.float32)
            outer = outer[:, low_col:low_col + slice_width].astype(jnp.float32)
            hidden = jax.nn.relu(jnp.dot(rows, inner)).astype(jnp.bfloat16)
            partial_value = jnp.dot(hidden.astype(jnp.float32), outer.T).astype(jnp.bfloat16)
            return lax.dynamic_update_slice_in_dim(buffer, partial_value, start, 0), None

        buffer = jnp.zeros((2 * TOKENS + most_rows, D), jnp.bfloat16)
        buffer, _ = lax.scan(per_expert, buffer, jnp.arange(EXPERTS, dtype=jnp.int32))
        assigned = jnp.zeros((2 * TOKENS, D), jnp.bfloat16).at[order].set(buffer[:2 * TOKENS])
        gated = (gates[:, :, None] * assigned.reshape(TOKENS, 2, D).astype(jnp.float32)).astype(jnp.bfloat16)
        gated = lax.optimization_barrier(gated)
        total = total + jnp.sum(gated.astype(jnp.float32), axis=1)
    return total.astype(jnp.bfloat16), placed_inner, placed_outer
```

```python
import functools

import jax
import jax.numpy as jnp
from jax import lax
from jax.experimental import pallas as pl
from jax.experimental.pallas import tpu as pltpu
from jax.sharding import PartitionSpec as P

F32 = jnp.float32
BF16 = jnp.bfloat16
EXTRA = 16


def params(mib=48):
    return pltpu.CompilerParams(vmem_limit_bytes=mib * 2**20)


def xor_permute(value, axis, mask):
    pairs = [(source, source ^ mask) for source in range(lax.axis_size(axis))]
    return lax.ppermute(value, axis, pairs)


def one_hot_slots(slots, rows, tokens):
    row = lax.broadcasted_iota(jnp.int32, (rows, tokens), 0).astype(F32)
    hit = (row == slots[0:1]) | (row == slots[1:2])
    return jnp.where(hit, 1.0, 0.0).astype(BF16)


def route_kernel(n_blocks, tok_dev, experts, per_expert, *refs):
    blocks = refs[:n_blocks]
    rows_ref, slots_ref, hot_ref = refs[n_blocks:]
    tokens = n_blocks * tok_dev

    @pl.when(pl.program_id(0) == 0)
    def _():
        tail = [b[tok_dev : tok_dev + EXTRA, 0:tok_dev].astype(F32) for b in blocks]
        info = jnp.concatenate(tail, axis=1)
        first, second = info[0:1], info[1:2]
        expert = lax.broadcasted_iota(jnp.int32, (experts, tokens), 0).astype(F32)
        is_first = expert == first
        is_second = expert == second
        named = jnp.where(is_first | is_second, 1.0, 0.0).astype(BF16)
        source = lax.broadcasted_iota(jnp.int32, (tokens, tokens), 0)
        target = lax.broadcasted_iota(jnp.int32, (tokens, tokens), 1)
        before = jnp.where(source < target, 1.0, 0.0).astype(BF16)
        rank = jnp.dot(named, before, preferred_element_type=F32)
        place = expert * float(per_expert) + rank
        slot_first = jnp.sum(jnp.where(is_first, place, 0.0), axis=0, keepdims=True)
        slot_second = jnp.sum(jnp.where(is_second, place, 0.0), axis=0, keepdims=True)
        slots = jnp.concatenate(
            [slot_first, slot_second, info[2:4], jnp.zeros((4, tokens), F32)], axis=0
        )
        slots_ref[...] = slots
        hot_ref[...] = one_hot_slots(slots, experts * per_expert, tokens)

    values = jnp.concatenate([b[0:tok_dev, :] for b in blocks], axis=0)
    rows_ref[...] = jnp.dot(hot_ref[...], values, preferred_element_type=F32).astype(BF16)


def route(blocks, experts, per_expert):
    n_blocks = len(blocks)
    tok_dev = blocks[0].shape[0] - EXTRA
    half = blocks[0].shape[1]
    tokens = n_blocks * tok_dev
    rows = experts * per_expert
    tile = 256
    return pl.pallas_call(
        functools.partial(route_kernel, n_blocks, tok_dev, experts, per_expert),
        grid=(half // tile,),
        in_specs=[pl.BlockSpec((tok_dev + EXTRA, tile), lambda i: (0, i))] * n_blocks,
        out_specs=[
            pl.BlockSpec((rows, tile), lambda i: (0, i)),
            pl.BlockSpec((8, tokens), lambda i: (0, 0)),
        ],
        out_shape=[
            jax.ShapeDtypeStruct((rows, half), BF16),
            jax.ShapeDtypeStruct((8, tokens), F32),
        ],
        scratch_shapes=[pltpu.VMEM((rows, tokens), BF16)],
        compiler_params=params(),
        cost_estimate=pl.CostEstimate(
            flops=2 * rows * tokens * half, bytes_accessed=2 * (rows + tokens) * half, transcendentals=0
        ),
        name="route",
    )(*blocks)


def fill_kernel(n_blocks, *refs):
    slots_ref = refs[0]
    blocks = refs[1 : 1 + n_blocks]
    rows_ref, hot_ref = refs[1 + n_blocks :]

    @pl.when(pl.program_id(0) == 0)
    def _():
        hot_ref[...] = one_hot_slots(slots_ref[...], hot_ref.shape[0], hot_ref.shape[1])

    values = jnp.concatenate([b[...] for b in blocks], axis=0)
    rows_ref[...] = jnp.dot(hot_ref[...], values, preferred_element_type=F32).astype(BF16)


def fill(slots, blocks, rows):
    n_blocks = len(blocks)
    tok_dev, half = blocks[0].shape
    tokens = n_blocks * tok_dev
    tile = 256
    return pl.pallas_call(
        functools.partial(fill_kernel, n_blocks),
        grid=(half // tile,),
        in_specs=[pl.BlockSpec((8, tokens), lambda i: (0, 0))]
        + [pl.BlockSpec((tok_dev, tile), lambda i: (0, i))] * n_blocks,
        out_specs=pl.BlockSpec((rows, tile), lambda i: (0, i)),
        out_shape=jax.ShapeDtypeStruct((rows, half), BF16),
        scratch_shapes=[pltpu.VMEM((rows, tokens), BF16)],
        compiler_params=params(),
        cost_estimate=pl.CostEstimate(
            flops=2 * rows * tokens * half, bytes_accessed=2 * (rows + tokens) * half, transcendentals=0
        ),
        name="fill",
    )(slots, *blocks)


def inner_kernel(low_ref, high_ref, inner_ref, outer_ref, hidden_ref, out_ref):
    half = low_ref.shape[1]
    total = jnp.dot(low_ref[...], inner_ref[0:half, :], preferred_element_type=F32)
    total += jnp.dot(high_ref[...], inner_ref[half : 2 * half, :], preferred_element_type=F32)
    hidden = jnp.maximum(total, 0.0).astype(BF16)
    hidden_ref[...] = hidden
    out_ref[...] = lax.dot_general(
        hidden, outer_ref[...], (((1,), (1,)), ((), ())), preferred_element_type=F32
    ).astype(BF16)


def feed_first(low, high, inner, outer):
    rows, half = low.shape
    units = inner.shape[1]
    tile = rows // 4
    return pl.pallas_call(
        inner_kernel,
        grid=(rows // tile,),
        in_specs=[
            pl.BlockSpec((tile, half), lambda i: (i, 0)),
            pl.BlockSpec((tile, half), lambda i: (i, 0)),
            pl.BlockSpec((2 * half, units), lambda i: (0, 0)),
            pl.BlockSpec((half, units), lambda i: (0, 0)),
        ],
        out_specs=[
            pl.BlockSpec((tile, units), lambda i: (i, 0)),
            pl.BlockSpec((tile, half), lambda i: (i, 0)),
        ],
        out_shape=[
            jax.ShapeDtypeStruct((rows, units), BF16),
            jax.ShapeDtypeStruct((rows, half), BF16),
        ],
        compiler_params=params(),
        cost_estimate=pl.CostEstimate(
            flops=6 * rows * half * units, bytes_accessed=2 * (4 * rows * half + 3 * half * units), transcendentals=0
        ),
        name="feed_first",
    )(low, high, inner, outer)


def outer_kernel(hidden_ref, outer_ref, out_ref):
    out_ref[...] = lax.dot_general(
        hidden_ref[...], outer_ref[...], (((1,), (1,)), ((), ())), preferred_element_type=F32
    ).astype(BF16)


def feed_second(hidden, outer, half):
    rows, units = hidden.shape
    tile = rows // 4
    return pl.pallas_call(
        outer_kernel,
        grid=(rows // tile,),
        in_specs=[
            pl.BlockSpec((tile, units), lambda i: (i, 0)),
            pl.BlockSpec((half, units), lambda i: (1, 0)),
        ],
        out_specs=pl.BlockSpec((tile, half), lambda i: (i, 0)),
        out_shape=jax.ShapeDtypeStruct((rows, half), BF16),
        compiler_params=params(),
        cost_estimate=pl.CostEstimate(
            flops=2 * rows * half * units, bytes_accessed=2 * (2 * rows * half + half * units), transcendentals=0
        ),
        name="feed_second",
    )(hidden, outer)


def combine_kernel(n_blocks, cols_ref, back_ref, *refs):
    outs = refs[:n_blocks]
    gate_ref = refs[n_blocks]
    tok_dev = outs[0].shape[0]

    @pl.when(pl.program_id(0) == 0)
    def _():
        cols = cols_ref[...]
        slot = lax.broadcasted_iota(jnp.int32, gate_ref.shape, 1).astype(F32)
        gate = jnp.where(slot == cols[:, 0:1], cols[:, 2:3], 0.0)
        gate = jnp.where(slot == cols[:, 1:2], cols[:, 3:4], gate)
        gate_ref[...] = (gate * (1.0 / 256.0)).astype(BF16)

    total = jnp.dot(gate_ref[...], back_ref[...], preferred_element_type=F32).astype(BF16)
    for block in range(n_blocks):
        outs[block][...] = total[block * tok_dev : (block + 1) * tok_dev, :]


def combine(cols, back, n_blocks, tok_dev):
    rows, half = back.shape
    tokens = n_blocks * tok_dev
    tile = 256
    return pl.pallas_call(
        functools.partial(combine_kernel, n_blocks),
        grid=(half // tile,),
        in_specs=[
            pl.BlockSpec((tokens, 8), lambda i: (0, 0)),
            pl.BlockSpec((rows, tile), lambda i: (0, i)),
        ],
        out_specs=[pl.BlockSpec((tok_dev, tile), lambda i: (0, i))] * n_blocks,
        out_shape=[jax.ShapeDtypeStruct((tok_dev, half), BF16)] * n_blocks,
        scratch_shapes=[pltpu.VMEM((tokens, rows), BF16)],
        compiler_params=params(),
        cost_estimate=pl.CostEstimate(
            flops=2 * rows * tokens * half, bytes_accessed=2 * (rows + tokens) * half, transcendentals=0
        ),
        name="combine",
    )(cols, back)


def trade(weight, flag, n_expert):
    return lax.cond(
        flag, lambda w: xor_permute(w, "expert", n_expert // 2), lambda w: w, weight
    )


def to_experts(rows, experts):
    count, half = rows.shape
    moved = lax.all_to_all(
        rows.reshape(experts, count // experts, half), "expert", split_axis=0, concat_axis=0, tiled=True
    )
    return moved.reshape(count, half)


def local(tokens, expert_ids, gate_levels, inner_weight, outer_weight, pair_flags):
    n_dp = lax.axis_size("dp")
    n_expert = lax.axis_size("expert")
    tok_dev, width = tokens.shape
    half = width // 2
    experts = n_expert * inner_weight.shape[0]
    capacity = max(2, 9 * tok_dev // (4 * experts))
    per_expert = n_dp * capacity
    rows = experts * per_expert
    flag = pair_flags[0] == 1

    routing = jnp.concatenate([expert_ids.T, gate_levels.T], axis=0).astype(BF16)
    routing = jnp.pad(routing, ((0, EXTRA - 4), (0, half - tok_dev)))
    low = jnp.concatenate([tokens[:, :half], routing], axis=0)
    high = tokens[:, half:]
    low_blocks = [low] + [xor_permute(low, "dp", s) for s in range(1, n_dp)]
    high_blocks = [high] + [xor_permute(high, "dp", s) for s in range(1, n_dp)]

    placed_inner = trade(inner_weight, flag, n_expert)
    *low_blocks, placed_inner = lax.optimization_barrier((*low_blocks, placed_inner))

    low_rows, slots = route(low_blocks, experts, per_expert)
    low_rows = to_experts(low_rows, experts)
    high_rows = fill(slots, high_blocks, rows)
    high_rows = to_experts(high_rows, experts)
    hidden, low_out = feed_first(low_rows, high_rows, inner_weight[0], outer_weight[0])
    low_back = to_experts(low_out, experts)
    high_out = feed_second(hidden, outer_weight[0], half)
    high_back = to_experts(high_out, experts)
    cols = slots.T
    low_parts = combine(cols, low_back, n_dp, tok_dev)
    high_parts = combine(cols, high_back, n_dp, tok_dev)

    *high_parts, late_outer = lax.optimization_barrier((*high_parts, outer_weight))
    placed_outer = trade(late_outer, flag, n_expert)

    def add_up(parts):
        total = parts[0].astype(F32)
        for s in range(1, n_dp):
            total = total + xor_permute(parts[s], "dp", s).astype(F32)
        return total.astype(BF16)

    mixture = jnp.concatenate([add_up(low_parts), add_up(high_parts)], axis=1)
    mixture, placed_outer = lax.optimization_barrier((mixture, placed_outer))
    return mixture, placed_inner, placed_outer


def solution(mesh):
    return jax.shard_map(
        local,
        mesh=mesh,
        in_specs=(
            P(("dp", "expert"), None),
            P(("dp", "expert"), None),
            P(("dp", "expert"), None),
            P("expert", None, "dp"),
            P("expert", None, "dp"),
            P("expert"),
        ),
        out_specs=(P(("dp", "expert"), None), P("expert", None, "dp"), P("expert", None, "dp")),
        check_vma=False,
    )
```

```python
import functools

import jax
import jax.numpy as jnp
from jax import lax
from jax.experimental import pallas as pl
from jax.experimental.pallas import tpu as pltpu
from jax.sharding import PartitionSpec as P

F32 = jnp.float32
BF16 = jnp.bfloat16
EXTRA = 16


def params(mib=48):
    return pltpu.CompilerParams(vmem_limit_bytes=mib * 2**20)


def cost(flops, values):
    return pl.CostEstimate(flops=flops, bytes_accessed=2 * values, transcendentals=0)


def xor_permute(value, axis, mask):
    pairs = [(source, source ^ mask) for source in range(lax.axis_size(axis))]
    return lax.ppermute(value, axis, pairs)


def rank_rows(first, second, experts):
    tokens = first.shape[1]
    expert = lax.broadcasted_iota(jnp.int32, (experts, tokens), 0).astype(F32)
    is_first, is_second = expert == first, expert == second
    named = jnp.where(is_first | is_second, 1.0, 0.0).astype(BF16)
    source = lax.broadcasted_iota(jnp.int32, (tokens, tokens), 0)
    target = lax.broadcasted_iota(jnp.int32, (tokens, tokens), 1)
    before = jnp.where(source < target, 1.0, 0.0).astype(BF16)
    rank = jnp.dot(named, before, preferred_element_type=F32)
    return expert, is_first, is_second, rank


def slot_rows(expert, is_first, is_second, rank, stride, base):
    place = expert * float(stride) + (rank + float(base))
    return (
        jnp.sum(jnp.where(is_first, place, 0.0), axis=0, keepdims=True),
        jnp.sum(jnp.where(is_second, place, 0.0), axis=0, keepdims=True),
    )


def one_hot(slot_first, slot_second, rows):
    row = lax.broadcasted_iota(jnp.int32, (rows, slot_first.shape[1]), 0).astype(F32)
    return jnp.where((row == slot_first) | (row == slot_second), 1.0, 0.0).astype(BF16)


def own_kernel(experts, slots, routing_ref, high_ref, rows_ref, hot_ref):
    @pl.when(pl.program_id(0) == 0)
    def _():
        info = routing_ref[...].astype(F32)
        ranks = rank_rows(info[0:1], info[1:2], experts)
        first, second = slot_rows(*ranks, slots, 0)
        hot_ref[...] = one_hot(first, second, experts * slots)

    picked = jnp.dot(hot_ref[...], high_ref[...], preferred_element_type=F32)
    rows_ref[...] = picked.reshape(rows_ref.shape).astype(BF16)


def own_rows(routing, high, experts, slots):
    tok_dev, width = high.shape
    tile = min(512, width)
    return pl.pallas_call(
        functools.partial(own_kernel, experts, slots),
        grid=(width // tile,),
        in_specs=[
            pl.BlockSpec(routing.shape, lambda i: (0, 0)),
            pl.BlockSpec((tok_dev, tile), lambda i: (0, i)),
        ],
        out_specs=pl.BlockSpec((experts, slots, tile), lambda i: (0, 0, i)),
        out_shape=jax.ShapeDtypeStruct((experts, slots, width), BF16),
        scratch_shapes=[pltpu.VMEM((experts * slots, tok_dev), BF16)],
        compiler_params=params(),
        cost_estimate=cost(2 * experts * slots * tok_dev * width, 4 * tok_dev * width),
        name="own_rows",
    )(routing, high)


def low_kernel(n, experts, slots, *refs):
    blocks = refs[:n]
    rows_ref, slots_ref, hot_ref = refs[n:]
    tok_dev = blocks[0].shape[0] - EXTRA

    @pl.when(pl.program_id(0) == 0)
    def _():
        parts = []
        for s in range(n):
            info = blocks[s][tok_dev : tok_dev + EXTRA, 0:tok_dev].astype(F32)
            ranks = rank_rows(info[0:1], info[1:2], experts)
            own = slot_rows(*ranks, slots, 0)
            full = slot_rows(*ranks, n * slots, s * slots)
            hot_ref[s] = one_hot(*own, experts * slots)
            parts.append(
                jnp.concatenate([*full, info[2:4], *own, jnp.zeros((2, tok_dev), F32)], axis=0)
            )
        slots_ref[...] = jnp.concatenate(parts, axis=1)

    for s in range(n):
        picked = jnp.dot(hot_ref[s], blocks[s][0:tok_dev, :], preferred_element_type=F32)
        rows_ref[:, s] = picked.reshape(experts, slots, picked.shape[1]).astype(BF16)


def low_rows(blocks, experts, slots):
    n = len(blocks)
    tok_dev, width = blocks[0].shape[0] - EXTRA, blocks[0].shape[1]
    tile = min(256, width)
    return pl.pallas_call(
        functools.partial(low_kernel, n, experts, slots),
        grid=(width // tile,),
        in_specs=[pl.BlockSpec((tok_dev + EXTRA, tile), lambda i: (0, i))] * n,
        out_specs=[
            pl.BlockSpec((experts, n, slots, tile), lambda i: (0, 0, 0, i)),
            pl.BlockSpec((8, n * tok_dev), lambda i: (0, 0)),
        ],
        out_shape=[
            jax.ShapeDtypeStruct((experts, n, slots, width), BF16),
            jax.ShapeDtypeStruct((8, n * tok_dev), F32),
        ],
        scratch_shapes=[pltpu.VMEM((n, experts * slots, tok_dev), BF16)],
        compiler_params=params(),
        cost_estimate=cost(2 * n * experts * slots * tok_dev * width, 4 * n * tok_dev * width),
        name="low_rows",
    )(*blocks)


def first_kernel(n, low_ref, *refs):
    highs = refs[:n]
    inner_ref, outer_ref, hidden_ref = refs[n : n + 3]
    outs = refs[n + 3 :]
    depth = low_ref.shape[3]

    def flat(value):
        rows = value.shape[0] * value.shape[1]
        return value.astype(F32).reshape(rows, value.shape[2]).astype(BF16)

    for s in range(n):

        @pl.when(pl.program_id(0) == s)
        def _(s=s):
            total = jnp.dot(flat(low_ref[:, 0]), inner_ref[0:depth, :], preferred_element_type=F32)
            total += jnp.dot(flat(highs[s][...]), inner_ref[depth:, :], preferred_element_type=F32)
            hidden = jnp.maximum(total, 0.0).astype(BF16)
            hidden_ref[0] = hidden
            out = lax.dot_general(
                hidden, outer_ref[...], (((1,), (1,)), ((), ())), preferred_element_type=F32
            )
            outs[s][...] = out.reshape(outs[s].shape).astype(BF16)


def feed_first(low, highs, inner, outer):
    experts, n, slots, depth = low.shape
    height = highs[0].shape[2]
    units = inner.shape[1]
    rows = experts * slots
    return pl.pallas_call(
        functools.partial(first_kernel, n),
        grid=(n,),
        in_specs=[pl.BlockSpec((experts, 1, slots, depth), lambda i: (0, i, 0, 0))]
        + [pl.BlockSpec((experts, slots, height), lambda i: (0, 0, 0))] * n
        + [
            pl.BlockSpec((depth + height, units), lambda i: (0, 0)),
            pl.BlockSpec((height, units), lambda i: (depth // height, 0)),
        ],
        out_specs=[pl.BlockSpec((1, rows, units), lambda i: (i, 0, 0))]
        + [pl.BlockSpec((experts, slots, height), lambda i: (0, 0, 0))] * n,
        out_shape=[jax.ShapeDtypeStruct((n, rows, units), BF16)]
        + [jax.ShapeDtypeStruct((experts, slots, height), BF16)] * n,
        compiler_params=params(),
        cost_estimate=cost(
            2 * n * rows * units * (depth + 2 * height), n * rows * 4 * height + units * (depth + 2 * height)
        ),
        name="feed_first",
    )(low, *highs, inner, outer)


def second_kernel(hidden_ref, outer_ref, out_ref):
    out = lax.dot_general(
        hidden_ref[0], outer_ref[...], (((1,), (1,)), ((), ())), preferred_element_type=F32
    )
    experts, _, slots, depth = out_ref.shape
    out_ref[:, 0] = out.reshape(experts, slots, depth).astype(BF16)


def feed_second(hidden, outer, experts, depth):
    n, rows, units = hidden.shape
    slots = rows // experts
    return pl.pallas_call(
        second_kernel,
        grid=(n,),
        in_specs=[
            pl.BlockSpec((1, rows, units), lambda i: (i, 0, 0)),
            pl.BlockSpec((depth, units), lambda i: (0, 0)),
        ],
        out_specs=pl.BlockSpec((experts, 1, slots, depth), lambda i: (0, i, 0, 0)),
        out_shape=jax.ShapeDtypeStruct((experts, n, slots, depth), BF16),
        compiler_params=params(),
        cost_estimate=cost(2 * n * rows * units * depth, 2 * n * rows * depth + units * depth),
        name="feed_second",
    )(hidden, outer)


def combine_kernel(n, first_col, cols_ref, back_ref, *refs):
    outs, gate_ref = refs[:n], refs[n]
    tok_dev = outs[0].shape[0]

    @pl.when(pl.program_id(0) == 0)
    def _():
        cols = cols_ref[...]
        slot = lax.broadcasted_iota(jnp.int32, gate_ref.shape, 1).astype(F32)
        gate = jnp.where(slot == cols[:, first_col : first_col + 1], cols[:, 2:3], 0.0)
        gate = jnp.where(slot == cols[:, first_col + 1 : first_col + 2], cols[:, 3:4], gate)
        gate_ref[...] = (gate * (1.0 / 256.0)).astype(BF16)

    total = jnp.dot(gate_ref[...], back_ref[...], preferred_element_type=F32).astype(BF16)
    for block in range(n):
        outs[block][...] = total[block * tok_dev : (block + 1) * tok_dev, :]


def combine(cols, back, n, tok_dev, first_col):
    rows, width = back.shape
    tokens = n * tok_dev
    tile = min(256, width)
    return pl.pallas_call(
        functools.partial(combine_kernel, n, first_col),
        grid=(width // tile,),
        in_specs=[
            pl.BlockSpec((tokens, 8), lambda i: (0, 0)),
            pl.BlockSpec((rows, tile), lambda i: (0, i)),
        ],
        out_specs=[pl.BlockSpec((tok_dev, tile), lambda i: (0, i))] * n,
        out_shape=[jax.ShapeDtypeStruct((tok_dev, width), BF16)] * n,
        scratch_shapes=[pltpu.VMEM((tokens, rows), BF16)],
        compiler_params=params(),
        cost_estimate=cost(2 * rows * tokens * width, (rows + tokens) * width),
        name="combine",
    )(cols, back)


def to_experts(rows):
    return lax.all_to_all(rows, "expert", split_axis=0, concat_axis=0, tiled=True)


def spread(value, n):
    return [value] + [xor_permute(value, "dp", s) for s in range(1, n)]


def add_up(parts):
    total = parts[0].astype(F32)
    for s in range(1, len(parts)):
        total = total + xor_permute(parts[s], "dp", s).astype(F32)
    return total.astype(BF16)


def with_trade(flag, weight, start, size, work, *operands):
    mask = lax.axis_size("expert") // 2

    def share(w):
        return lax.slice_in_dim(w, start, start + size, axis=1)

    def trading(w, *values):
        return xor_permute(share(w), "expert", mask), work(*values)

    def staying(w, *values):
        return share(w), work(*values)

    return lax.cond(flag, trading, staying, weight, *operands)


def after(value, *others):
    return lax.optimization_barrier((value, *others))[0]


def local(tokens, expert_ids, gate_levels, inner_weight, outer_weight, pair_flags):
    n_dp = lax.axis_size("dp")
    n_expert = lax.axis_size("expert")
    tok_dev, width = tokens.shape
    depth = width // 2
    experts = n_expert * inner_weight.shape[0]
    capacity = max(2, 9 * tok_dev // (4 * experts))
    slots = -(-capacity // 8) * 8
    flag = pair_flags[0] == 1
    share = inner_weight.shape[1] // 2

    routing = jnp.concatenate([expert_ids.T, gate_levels.T], axis=0).astype(BF16)
    routing = jnp.pad(routing, ((0, EXTRA - 4), (0, 0)))
    low = jnp.concatenate(
        [tokens[:, :depth], jnp.pad(routing, ((0, 0), (0, depth - tok_dev)))], axis=0
    )
    own = own_rows(routing, tokens[:, depth:], experts, slots)
    high = to_experts(own)

    inner_a, (rows, info) = with_trade(
        after(flag, own), inner_weight, 0, share,
        lambda low: tuple(low_rows(spread(low, n_dp), experts, slots)), low,
    )
    moved = to_experts(rows.reshape(experts, n_dp * slots, depth)).reshape(rows.shape)
    inner_b, highs = with_trade(
        after(flag, rows), inner_weight, share, share, lambda high: tuple(spread(high, n_dp)), high
    )
    hidden, *out_highs = feed_first(moved, highs, inner_weight[0], outer_weight[0])
    out_low = feed_second(hidden, outer_weight[0], experts, depth)
    back = to_experts(out_low.reshape(experts, n_dp * slots, depth))
    outer_a, summed = with_trade(
        after(flag, out_low), outer_weight, 0, share, lambda *parts: add_up(parts), *out_highs
    )
    cols = info.T
    parts = combine(cols, back.reshape(experts * n_dp * slots, depth), n_dp, tok_dev, 0)
    back_own = to_experts(after(summed, parts[0]))
    outer_b, mixed_low = with_trade(
        after(flag, summed, parts[0]), outer_weight, share, share, lambda *parts: add_up(parts), *parts
    )
    [mixed_high] = combine(
        cols[0:tok_dev], back_own.reshape(experts * slots, width - depth), 1, tok_dev, 4
    )
    mixture = jnp.concatenate([mixed_low, mixed_high], axis=1)
    placed_inner = jnp.concatenate([inner_a, inner_b], axis=1)
    placed_outer = jnp.concatenate([outer_a, outer_b], axis=1)
    return mixture, placed_inner, placed_outer


def solution(mesh):
    return jax.shard_map(
        local,
        mesh=mesh,
        in_specs=(
            P(("dp", "expert"), None),
            P(("dp", "expert"), None),
            P(("dp", "expert"), None),
            P("expert", None, "dp"),
            P("expert", None, "dp"),
            P("expert"),
        ),
        out_specs=(P(("dp", "expert"), None), P("expert", None, "dp"), P("expert", None, "dp")),
        check_vma=False,
    )
```

```python
import functools

import jax
import jax.numpy as jnp
from jax import lax
from jax.experimental import pallas as pl
from jax.experimental.pallas import tpu as pltpu
from jax.sharding import PartitionSpec as P

F32 = jnp.float32
BF16 = jnp.bfloat16
EXTRA = 16


def params(mib=48):
    return pltpu.CompilerParams(vmem_limit_bytes=mib * 2**20)


def cost(flops, values):
    return pl.CostEstimate(flops=flops, bytes_accessed=2 * values, transcendentals=0)


def xor_permute(value, axis, mask):
    pairs = [(source, source ^ mask) for source in range(lax.axis_size(axis))]
    return lax.ppermute(value, axis, pairs)


def rank_rows(first, second, experts):
    tokens = first.shape[1]
    expert = lax.broadcasted_iota(jnp.int32, (experts, tokens), 0).astype(F32)
    is_first, is_second = expert == first, expert == second
    named = jnp.where(is_first | is_second, 1.0, 0.0).astype(BF16)
    source = lax.broadcasted_iota(jnp.int32, (tokens, tokens), 0)
    target = lax.broadcasted_iota(jnp.int32, (tokens, tokens), 1)
    before = jnp.where(source < target, 1.0, 0.0).astype(BF16)
    rank = jnp.dot(named, before, preferred_element_type=F32)
    return expert, is_first, is_second, rank


def slot_rows(expert, is_first, is_second, rank, stride, base):
    place = expert * float(stride) + (rank + float(base))
    return (
        jnp.sum(jnp.where(is_first, place, 0.0), axis=0, keepdims=True),
        jnp.sum(jnp.where(is_second, place, 0.0), axis=0, keepdims=True),
    )


def one_hot(slot_first, slot_second, rows):
    row = lax.broadcasted_iota(jnp.int32, (rows, slot_first.shape[1]), 0).astype(F32)
    return jnp.where((row == slot_first) | (row == slot_second), 1.0, 0.0).astype(BF16)


def own_kernel(experts, slots, routing_ref, high_ref, rows_ref, hot_ref):
    @pl.when(pl.program_id(0) == 0)
    def _():
        info = routing_ref[...].astype(F32)
        ranks = rank_rows(info[0:1], info[1:2], experts)
        first, second = slot_rows(*ranks, slots, 0)
        hot_ref[...] = one_hot(first, second, experts * slots)

    picked = jnp.dot(hot_ref[...], high_ref[...], preferred_element_type=F32)
    rows_ref[...] = picked.reshape(rows_ref.shape).astype(BF16)


def own_rows(routing, high, experts, slots):
    tok_dev, width = high.shape
    tile = min(512, width)
    return pl.pallas_call(
        functools.partial(own_kernel, experts, slots),
        grid=(width // tile,),
        in_specs=[
            pl.BlockSpec(routing.shape, lambda i: (0, 0)),
            pl.BlockSpec((tok_dev, tile), lambda i: (0, i)),
        ],
        out_specs=pl.BlockSpec((experts, slots, tile), lambda i: (0, 0, i)),
        out_shape=jax.ShapeDtypeStruct((experts, slots, width), BF16),
        scratch_shapes=[pltpu.VMEM((experts * slots, tok_dev), BF16)],
        compiler_params=params(),
        cost_estimate=cost(2 * experts * slots * tok_dev * width, 4 * tok_dev * width),
        name="own_rows",
    )(routing, high)


def low_kernel(n, experts, slots, *refs):
    blocks = refs[:n]
    rows_ref, slots_ref, hot_ref = refs[n:]
    tok_dev = blocks[0].shape[0] - EXTRA

    @pl.when(pl.program_id(0) == 0)
    def _():
        parts = []
        for s in range(n):
            info = blocks[s][tok_dev : tok_dev + EXTRA, 0:tok_dev].astype(F32)
            ranks = rank_rows(info[0:1], info[1:2], experts)
            own = slot_rows(*ranks, slots, 0)
            full = slot_rows(*ranks, n * slots, s * slots)
            hot_ref[s] = one_hot(*own, experts * slots)
            parts.append(
                jnp.concatenate([*full, info[2:4], *own, jnp.zeros((2, tok_dev), F32)], axis=0)
            )
        slots_ref[...] = jnp.concatenate(parts, axis=1)

    for s in range(n):
        picked = jnp.dot(hot_ref[s], blocks[s][0:tok_dev, :], preferred_element_type=F32)
        rows_ref[:, s] = picked.reshape(experts, slots, picked.shape[1]).astype(BF16)


def low_rows(blocks, experts, slots):
    n = len(blocks)
    tok_dev, width = blocks[0].shape[0] - EXTRA, blocks[0].shape[1]
    tile = min(256, width)
    return pl.pallas_call(
        functools.partial(low_kernel, n, experts, slots),
        grid=(width // tile,),
        in_specs=[pl.BlockSpec((tok_dev + EXTRA, tile), lambda i: (0, i))] * n,
        out_specs=[
            pl.BlockSpec((experts, n, slots, tile), lambda i: (0, 0, 0, i)),
            pl.BlockSpec((8, n * tok_dev), lambda i: (0, 0)),
        ],
        out_shape=[
            jax.ShapeDtypeStruct((experts, n, slots, width), BF16),
            jax.ShapeDtypeStruct((8, n * tok_dev), F32),
        ],
        scratch_shapes=[pltpu.VMEM((n, experts * slots, tok_dev), BF16)],
        compiler_params=params(),
        cost_estimate=cost(2 * n * experts * slots * tok_dev * width, 4 * n * tok_dev * width),
        name="low_rows",
    )(*blocks)


def feed_kernel(n, low_ref, *refs):
    highs = refs[:n]
    inner_ref, outer_ref = refs[n : n + 2]
    low_out_ref, outs = refs[-n - 1], refs[-n:]
    depth = low_ref.shape[3]

    def flat(value):
        rows = value.shape[0] * value.shape[1]
        return value.astype(F32).reshape(rows, value.shape[2]).astype(BF16)

    def outer_dot(hidden, start, size):
        return lax.dot_general(
            hidden, outer_ref[start : start + size, :], (((1,), (1,)), ((), ())),
            preferred_element_type=F32,
        )

    for s in range(n):

        @pl.when(pl.program_id(0) == s)
        def _(s=s):
            total = jnp.dot(flat(low_ref[:, 0]), inner_ref[0:depth, :], preferred_element_type=F32)
            total += jnp.dot(flat(highs[s][...]), inner_ref[depth:, :], preferred_element_type=F32)
            hidden = jnp.maximum(total, 0.0).astype(BF16)
            experts, slots, height = outs[s].shape
            out = outer_dot(hidden, depth, height)
            outs[s][...] = out.reshape(experts, slots, height).astype(BF16)
            out = outer_dot(hidden, 0, depth)
            low_out_ref[:, 0] = out.reshape(experts, slots, depth).astype(BF16)


def feed(low, base, highs, inner, outer, *earlier):
    experts, blocks, slots, depth = low.shape
    n = len(highs)
    height = highs[0].shape[2]
    units = inner.shape[1]
    rows = n * experts * slots
    whole = pl.BlockSpec((experts, slots, height), lambda i: (0, 0, 0))
    return pl.pallas_call(
        functools.partial(feed_kernel, n),
        grid=(n,),
        in_specs=[pl.BlockSpec((experts, 1, slots, depth), lambda i: (0, base + i, 0, 0))]
        + [whole] * n
        + [pl.BlockSpec((depth + height, units), lambda i: (0, 0))] * 2
        + [pl.BlockSpec(memory_space=pl.ANY)] * len(earlier),
        out_specs=[pl.BlockSpec((experts, 1, slots, depth), lambda i: (0, base + i, 0, 0))]
        + [whole] * n,
        input_output_aliases={n + 3: 0} if earlier else {},
        out_shape=[jax.ShapeDtypeStruct((experts, blocks, slots, depth), BF16)]
        + [jax.ShapeDtypeStruct((experts, slots, height), BF16)] * n,
        compiler_params=params(),
        cost_estimate=cost(4 * rows * units * (depth + height), 2 * (rows + units) * (depth + height)),
        name="feed",
    )(low, *highs, inner, outer, *earlier)


def combine_kernel(n, first_col, cols_ref, back_ref, *refs):
    outs, gate_ref = refs[:n], refs[n]
    tok_dev = outs[0].shape[0]

    @pl.when(pl.program_id(0) == 0)
    def _():
        cols = cols_ref[...]
        slot = lax.broadcasted_iota(jnp.int32, gate_ref.shape, 1).astype(F32)
        gate = jnp.where(slot == cols[:, first_col : first_col + 1], cols[:, 2:3], 0.0)
        gate = jnp.where(slot == cols[:, first_col + 1 : first_col + 2], cols[:, 3:4], gate)
        gate_ref[...] = (gate * (1.0 / 256.0)).astype(BF16)

    total = jnp.dot(gate_ref[...], back_ref[...], preferred_element_type=F32).astype(BF16)
    for block in range(n):
        outs[block][...] = total[block * tok_dev : (block + 1) * tok_dev, :]


def combine(cols, back, n, tok_dev, first_col):
    rows, width = back.shape
    tokens = n * tok_dev
    tile = min(256, width)
    return pl.pallas_call(
        functools.partial(combine_kernel, n, first_col),
        grid=(width // tile,),
        in_specs=[
            pl.BlockSpec((tokens, 8), lambda i: (0, 0)),
            pl.BlockSpec((rows, tile), lambda i: (0, i)),
        ],
        out_specs=[pl.BlockSpec((tok_dev, tile), lambda i: (0, i))] * n,
        out_shape=[jax.ShapeDtypeStruct((tok_dev, width), BF16)] * n,
        scratch_shapes=[pltpu.VMEM((tokens, rows), BF16)],
        compiler_params=params(),
        cost_estimate=cost(2 * rows * tokens * width, (rows + tokens) * width),
        name="combine",
    )(cols, back)


def to_experts(rows):
    return lax.all_to_all(rows, "expert", split_axis=0, concat_axis=0, tiled=True)


def add_up(parts):
    total = parts[0].astype(F32)
    for part in parts[1:]:
        total = total + part.astype(F32)
    return total.astype(BF16)


def fetch(parts, base):
    return [xor_permute(part, "dp", base + s) for s, part in enumerate(parts)]


def share_of(weight, start, size):
    return lax.slice_in_dim(weight, start, start + size, axis=1)


def with_trade(flag, weight, start, size, work, *operands):
    mask = lax.axis_size("expert") // 2

    def trading(w, *values):
        return xor_permute(share_of(w, start, size), "expert", mask), work(*values)

    def staying(w, *values):
        return share_of(w, start, size), work(*values)

    return lax.cond(flag, trading, staying, weight, *operands)


def with_last_trade(flag, weight, start, placed, work, *operands):
    mask = lax.axis_size("expert") // 2
    size = weight.shape[1] - start

    def base(w, placed):
        both = jnp.concatenate([placed, share_of(w, start, size)], axis=1)
        return lax.optimization_barrier(both)

    def trading(w, placed, *values):
        moved = xor_permute(share_of(w, start, size), "expert", mask)
        result = work(*values)
        return lax.dynamic_update_slice_in_dim(base(w, placed), moved, start, axis=1), result

    def staying(w, placed, *values):
        return base(w, placed), work(*values)

    return lax.cond(flag, trading, staying, weight, placed, *operands)


def after(value, *others):
    return lax.optimization_barrier((value, *others))[0]


def local(tokens, expert_ids, gate_levels, inner_weight, outer_weight, pair_flags):
    n_dp = lax.axis_size("dp")
    n_expert = lax.axis_size("expert")
    tok_dev, width = tokens.shape
    depth = width // 2
    experts = n_expert * inner_weight.shape[0]
    capacity = max(2, 9 * tok_dev // (4 * experts))
    slots = -(-capacity // 8) * 8
    group = n_dp // 2
    flag = pair_flags[0] == 1
    share = inner_weight.shape[1] // 2
    inner, outer = inner_weight[0], outer_weight[0]

    routing = jnp.concatenate([expert_ids.T, gate_levels.T], axis=0).astype(BF16)
    routing = jnp.pad(routing, ((0, EXTRA - 4), (0, 0)))
    low = jnp.concatenate(
        [tokens[:, :depth], jnp.pad(routing, ((0, 0), (0, depth - tok_dev)))], axis=0
    )
    own = own_rows(routing, tokens[:, depth:], experts, slots)
    high = to_experts(own)

    inner_a, (rows, info) = with_trade(
        after(flag, own), inner_weight, 0, share,
        lambda low: tuple(low_rows([low, *fetch([low] * (n_dp - 1), 1)], experts, slots)), low,
    )
    moved = to_experts(rows.reshape(experts, n_dp * slots, depth)).reshape(rows.shape)
    highs = [high, *fetch([high] * (n_dp - 1), 1)]

    def first_half(moved, inner, outer, *highs):
        return tuple(feed(moved, 0, highs, inner, outer))

    inner_b, (low_a, *high_a) = with_trade(
        flag, inner_weight, share, share, first_half, moved, inner, outer, *highs[:group]
    )
    got_a = fetch(high_a[1:], 1)
    *later, low_a = lax.optimization_barrier((*highs[group:], low_a))
    out_low, *high_b = feed(moved, group, later, inner, outer, low_a)
    back = to_experts(out_low.reshape(experts, n_dp * slots, depth))

    def third(inner_a, inner_b, *high_b):
        return tuple(fetch(high_b, group)), jnp.concatenate([inner_a, inner_b], axis=1)

    outer_a, (got_b, placed_inner) = with_trade(
        after(flag, out_low), outer_weight, 0, share, third, inner_a, inner_b, *high_b
    )
    summed = add_up([high_a[0], *got_a, *got_b])
    cols = info.T
    parts = combine(cols, back.reshape(experts * n_dp * slots, depth), n_dp, tok_dev, 0)
    back_own = to_experts(after(summed, parts[0]))
    placed_outer, mixed_low = with_last_trade(
        after(flag, summed, parts[0]), outer_weight, share, outer_a,
        lambda *parts: add_up([parts[0], *fetch(parts[1:], 1)]), *parts,
    )
    [mixed_high] = combine(
        cols[0:tok_dev], back_own.reshape(experts * slots, width - depth), 1, tok_dev, 4
    )
    mixture = jnp.concatenate([mixed_low, mixed_high], axis=1)
    return mixture, placed_inner, placed_outer


def solution(mesh):
    return jax.shard_map(
        local,
        mesh=mesh,
        in_specs=(
            P(("dp", "expert"), None),
            P(("dp", "expert"), None),
            P(("dp", "expert"), None),
            P("expert", None, "dp"),
            P("expert", None, "dp"),
            P("expert"),
        ),
        out_specs=(P(("dp", "expert"), None), P("expert", None, "dp"), P("expert", None, "dp")),
        check_vma=False,
    )
```

```python
import functools

import jax
import jax.numpy as jnp
from jax import lax
from jax.experimental import pallas as pl
from jax.experimental.pallas import tpu as pltpu
from jax.sharding import PartitionSpec as P

F32 = jnp.float32
BF16 = jnp.bfloat16
CUTS = (6, 11, 8)
EXTRA = 16


def params(mib=48):
    return pltpu.CompilerParams(vmem_limit_bytes=mib * 2**20)


def cost(flops, values):
    return pl.CostEstimate(flops=flops, bytes_accessed=2 * values, transcendentals=0)


def xor_permute(value, axis, mask):
    pairs = [(source, source ^ mask) for source in range(lax.axis_size(axis))]
    return lax.ppermute(value, axis, pairs)


def rank_rows(first, second, experts):
    tokens = first.shape[1]
    expert = lax.broadcasted_iota(jnp.int32, (experts, tokens), 0).astype(F32)
    is_first, is_second = expert == first, expert == second
    named = jnp.where(is_first | is_second, 1.0, 0.0).astype(BF16)
    source = lax.broadcasted_iota(jnp.int32, (tokens, tokens), 0)
    target = lax.broadcasted_iota(jnp.int32, (tokens, tokens), 1)
    before = jnp.where(source < target, 1.0, 0.0).astype(BF16)
    rank = jnp.dot(named, before, preferred_element_type=F32)
    return expert, is_first, is_second, rank


def slot_rows(expert, is_first, is_second, rank, stride, base):
    place = expert * float(stride) + (rank + float(base))
    return (
        jnp.sum(jnp.where(is_first, place, 0.0), axis=0, keepdims=True),
        jnp.sum(jnp.where(is_second, place, 0.0), axis=0, keepdims=True),
    )


def one_hot(slot_first, slot_second, rows):
    row = lax.broadcasted_iota(jnp.int32, (rows, slot_first.shape[1]), 0).astype(F32)
    return jnp.where((row == slot_first) | (row == slot_second), 1.0, 0.0).astype(BF16)


def own_kernel(experts, slots, routing_ref, high_ref, rows_ref, hot_ref):
    @pl.when(pl.program_id(0) == 0)
    def _():
        info = routing_ref[...].astype(F32)
        ranks = rank_rows(info[0:1], info[1:2], experts)
        first, second = slot_rows(*ranks, slots, 0)
        hot_ref[...] = one_hot(first, second, experts * slots)

    picked = jnp.dot(hot_ref[...], high_ref[...], preferred_element_type=F32)
    rows_ref[...] = picked.reshape(rows_ref.shape).astype(BF16)


def own_rows(routing, high, experts, slots):
    tok_dev, width = high.shape
    tile = min(512, width)
    return pl.pallas_call(
        functools.partial(own_kernel, experts, slots),
        grid=(width // tile,),
        in_specs=[
            pl.BlockSpec(routing.shape, lambda i: (0, 0)),
            pl.BlockSpec((tok_dev, tile), lambda i: (0, i)),
        ],
        out_specs=pl.BlockSpec((experts, slots, tile), lambda i: (0, 0, i)),
        out_shape=jax.ShapeDtypeStruct((experts, slots, width), BF16),
        scratch_shapes=[pltpu.VMEM((experts * slots, tok_dev), BF16)],
        compiler_params=params(),
        cost_estimate=cost(2 * experts * slots * tok_dev * width, 4 * tok_dev * width),
        name="own_rows",
    )(routing, high)


def low_kernel(n, experts, slots, *refs):
    blocks = refs[:n]
    rows_ref, slots_ref, hot_ref = refs[n:]
    tok_dev = blocks[0].shape[0] - EXTRA

    @pl.when(pl.program_id(0) == 0)
    def _():
        parts = []
        for s in range(n):
            info = blocks[s][tok_dev : tok_dev + EXTRA, 0:tok_dev].astype(F32)
            ranks = rank_rows(info[0:1], info[1:2], experts)
            own = slot_rows(*ranks, slots, 0)
            full = slot_rows(*ranks, n * slots, s * slots)
            hot_ref[s] = one_hot(*own, experts * slots)
            parts.append(
                jnp.concatenate([*full, info[2:4], *own, jnp.zeros((2, tok_dev), F32)], axis=0)
            )
        slots_ref[...] = jnp.concatenate(parts, axis=1)

    for s in range(n):
        picked = jnp.dot(hot_ref[s], blocks[s][0:tok_dev, :], preferred_element_type=F32)
        rows_ref[:, s] = picked.reshape(experts, slots, picked.shape[1]).astype(BF16)


def low_rows(blocks, experts, slots):
    n = len(blocks)
    tok_dev, width = blocks[0].shape[0] - EXTRA, blocks[0].shape[1]
    tile = min(256, width)
    return pl.pallas_call(
        functools.partial(low_kernel, n, experts, slots),
        grid=(width // tile,),
        in_specs=[pl.BlockSpec((tok_dev + EXTRA, tile), lambda i: (0, i))] * n,
        out_specs=[
            pl.BlockSpec((experts, n, slots, tile), lambda i: (0, 0, 0, i)),
            pl.BlockSpec((8, n * tok_dev), lambda i: (0, 0)),
        ],
        out_shape=[
            jax.ShapeDtypeStruct((experts, n, slots, width), BF16),
            jax.ShapeDtypeStruct((8, n * tok_dev), F32),
        ],
        scratch_shapes=[pltpu.VMEM((n, experts * slots, tok_dev), BF16)],
        compiler_params=params(),
        cost_estimate=cost(40 * n * experts * slots * tok_dev * width, 100 * n * tok_dev * width),
        name="low_rows",
    )(*blocks)


def feed_kernel(n, low_ref, *refs):
    highs = refs[:n]
    inner_ref, outer_ref = refs[n : n + 2]
    low_out_ref, outs = refs[-n - 1], refs[-n:]
    depth = low_ref.shape[3]

    def flat(value):
        rows = value.shape[0] * value.shape[1]
        return value.astype(F32).reshape(rows, value.shape[2]).astype(BF16)

    def outer_dot(hidden, start, size):
        return lax.dot_general(
            hidden, outer_ref[start : start + size, :], (((1,), (1,)), ((), ())),
            preferred_element_type=F32,
        )

    for s in range(n):

        @pl.when(pl.program_id(0) == s)
        def _(s=s):
            total = jnp.dot(flat(low_ref[:, 0]), inner_ref[0:depth, :], preferred_element_type=F32)
            total += jnp.dot(flat(highs[s][...]), inner_ref[depth:, :], preferred_element_type=F32)
            hidden = jnp.maximum(total, 0.0).astype(BF16)
            experts, slots, height = outs[s].shape
            out = outer_dot(hidden, depth, height)
            outs[s][...] = out.reshape(experts, slots, height).astype(BF16)
            out = outer_dot(hidden, 0, depth)
            low_out_ref[:, 0] = out.reshape(experts, slots, depth).astype(BF16)


def feed(low, base, highs, inner, outer, *earlier):
    experts, blocks, slots, depth = low.shape
    n = len(highs)
    height = highs[0].shape[2]
    units = inner.shape[1]
    rows = n * experts * slots
    whole = pl.BlockSpec((experts, slots, height), lambda i: (0, 0, 0))
    return pl.pallas_call(
        functools.partial(feed_kernel, n),
        grid=(n,),
        in_specs=[pl.BlockSpec((experts, 1, slots, depth), lambda i: (0, base + i, 0, 0))]
        + [whole] * n
        + [pl.BlockSpec((depth + height, units), lambda i: (0, 0))] * 2
        + [pl.BlockSpec(memory_space=pl.ANY)] * len(earlier),
        out_specs=[pl.BlockSpec((experts, 1, slots, depth), lambda i: (0, base + i, 0, 0))]
        + [whole] * n,
        input_output_aliases={n + 3: 0} if earlier else {},
        out_shape=[jax.ShapeDtypeStruct((experts, blocks, slots, depth), BF16)]
        + [jax.ShapeDtypeStruct((experts, slots, height), BF16)] * n,
        compiler_params=params(),
        cost_estimate=cost(4 * rows * units * (depth + height), 2 * (rows + units) * (depth + height)),
        name="feed",
    )(low, *highs, inner, outer, *earlier)


def combine_kernel(n, first_col, cols_ref, back_ref, *refs):
    outs, gate_ref = refs[:n], refs[n]
    tok_dev = outs[0].shape[0]

    @pl.when(pl.program_id(0) == 0)
    def _():
        cols = cols_ref[...]
        slot = lax.broadcasted_iota(jnp.int32, gate_ref.shape, 1).astype(F32)
        gate = jnp.where(slot == cols[:, first_col : first_col + 1], cols[:, 2:3], 0.0)
        gate = jnp.where(slot == cols[:, first_col + 1 : first_col + 2], cols[:, 3:4], gate)
        gate_ref[...] = (gate * (1.0 / 256.0)).astype(BF16)

    total = jnp.dot(gate_ref[...], back_ref[...], preferred_element_type=F32).astype(BF16)
    for block in range(n):
        outs[block][...] = total[block * tok_dev : (block + 1) * tok_dev, :]


def combine(cols, back, n, tok_dev, first_col):
    rows, width = back.shape
    tokens = n * tok_dev
    tile = min(256, width)
    return pl.pallas_call(
        functools.partial(combine_kernel, n, first_col),
        grid=(width // tile,),
        in_specs=[
            pl.BlockSpec((tokens, 8), lambda i: (0, 0)),
            pl.BlockSpec((rows, tile), lambda i: (0, i)),
        ],
        out_specs=[pl.BlockSpec((tok_dev, tile), lambda i: (0, i))] * n,
        out_shape=[jax.ShapeDtypeStruct((tok_dev, width), BF16)] * n,
        scratch_shapes=[pltpu.VMEM((tokens, rows), BF16)],
        compiler_params=params(),
        cost_estimate=cost(2 * rows * tokens * width, (rows + tokens) * width),
        name="combine",
    )(cols, back)


def to_experts(rows):
    return lax.all_to_all(rows, "expert", split_axis=0, concat_axis=0, tiled=True)


def add_up(parts):
    total = parts[0].astype(F32)
    for part in parts[1:]:
        total = total + part.astype(F32)
    return total.astype(BF16)


def fetch(parts, base):
    return [xor_permute(part, "dp", base + s) for s, part in enumerate(parts)]


def spread(value, n):
    values = [value]
    for s in range(1, n):
        values.append(xor_permute(values[s & (s - 1)], "dp", s & -s))
    return values


def fold(parts):
    parts = list(parts)
    for s in range(len(parts) - 1, 0, -1):
        rest = s & (s - 1)
        parts[rest] = add_up([parts[rest], xor_permute(parts[s], "dp", s & -s)])
    return parts[0]


def share_of(weight, start, size):
    return lax.slice_in_dim(weight, start, start + size, axis=1)


def with_trade(flag, weight, start, size, work, *operands):
    mask = lax.axis_size("expert") // 2

    def trading(w, *values):
        return xor_permute(share_of(w, start, size), "expert", mask), work(*values)

    def staying(w, *values):
        return share_of(w, start, size), work(*values)

    return lax.cond(flag, trading, staying, weight, *operands)


def with_last_trade(flag, weight, start, placed, work, *operands):
    mask = lax.axis_size("expert") // 2
    size = weight.shape[1] - start

    def base(w, placed):
        both = jnp.concatenate([placed, share_of(w, start, size)], axis=1)
        return lax.optimization_barrier(both)

    def trading(w, placed, *values):
        moved = xor_permute(share_of(w, start, size), "expert", mask)
        result = work(*values)
        return lax.dynamic_update_slice_in_dim(base(w, placed), moved, start, axis=1), result

    def staying(w, placed, *values):
        return base(w, placed), work(*values)

    return lax.cond(flag, trading, staying, weight, placed, *operands)


def after(value, *others):
    return lax.optimization_barrier((value, *others))[0]


def local(tokens, expert_ids, gate_levels, inner_weight, outer_weight, pair_flags):
    n_dp = lax.axis_size("dp")
    n_expert = lax.axis_size("expert")
    tok_dev, width = tokens.shape
    depth = width // 2
    experts = n_expert * inner_weight.shape[0]
    capacity = max(2, 9 * tok_dev // (4 * experts))
    slots = -(-capacity // 8) * 8
    group = n_dp // 2
    flag = pair_flags[0] == 1
    rows_in = inner_weight.shape[1]
    cut_a, cut_b = rows_in * CUTS[0] // 16, rows_in * CUTS[1] // 16
    share = rows_in * CUTS[2] // 16
    inner, outer = inner_weight[0], outer_weight[0]

    routing = jnp.concatenate([expert_ids.T, gate_levels.T], axis=0).astype(BF16)
    routing = jnp.pad(routing, ((0, EXTRA - 4), (0, 0)))
    low = jnp.concatenate(
        [tokens[:, :depth], jnp.pad(routing, ((0, 0), (0, depth - tok_dev)))], axis=0
    )
    own = own_rows(routing, tokens[:, depth:], experts, slots)
    high = to_experts(own)

    lows = [low, *fetch([low] * (n_dp - 1), 1)]
    inner_a, _ = with_trade(after(flag, own), inner_weight, 0, cut_a, lambda: ())
    high, inner_a = lax.optimization_barrier((high, inner_a))
    *lows, inner_a = lax.optimization_barrier((*lows, inner_a))
    rows, info = low_rows(lows, experts, slots)
    moved = to_experts(rows.reshape(experts, n_dp * slots, depth)).reshape(rows.shape)
    highs = spread(high, n_dp)

    def first_half(moved, inner, outer, *highs):
        return tuple(feed(moved, 0, highs, inner, outer))

    inner_b, (low_a, *high_a) = with_trade(
        flag, inner_weight, cut_a, cut_b - cut_a, first_half, moved, inner, outer, *highs[:group]
    )
    *later, low_a = lax.optimization_barrier((*highs[group:], low_a))

    def second_half(moved, inner, outer, low_a, *highs):
        done, sent = highs[: n_dp - group], highs[n_dp - group :]
        return tuple(feed(moved, group, done, inner, outer, low_a)), fold(sent)

    inner_c, ((out_low, *high_b), folded) = with_trade(
        flag, inner_weight, cut_b, rows_in - cut_b, second_half,
        moved, inner, outer, low_a, *later, *high_a,
    )
    back = to_experts(out_low.reshape(experts, n_dp * slots, depth))

    def third(inner_a, inner_b, inner_c, *high_b):
        got = xor_permute(fold(high_b), "dp", group)
        return got, jnp.concatenate([inner_a, inner_b, inner_c], axis=1)

    outer_a, (got, placed_inner) = with_trade(
        after(flag, out_low), outer_weight, 0, share, third, inner_a, inner_b, inner_c, *high_b
    )
    summed = add_up([folded, got])
    cols = info.T
    parts = combine(cols, back.reshape(experts * n_dp * slots, depth), n_dp, tok_dev, 0)
    back_own = to_experts(after(summed, parts[0]))
    placed_outer, mixed_low = with_last_trade(
        after(flag, summed, parts[0]), outer_weight, share, outer_a,
        lambda *parts: add_up([parts[0], *fetch(parts[1:], 1)]), *parts,
    )
    [mixed_high] = combine(
        cols[0:tok_dev], back_own.reshape(experts * slots, width - depth), 1, tok_dev, 4
    )
    mixture = jnp.concatenate([mixed_low, mixed_high], axis=1)
    return mixture, placed_inner, placed_outer


def solution(mesh):
    return jax.shard_map(
        local,
        mesh=mesh,
        in_specs=(
            P(("dp", "expert"), None),
            P(("dp", "expert"), None),
            P(("dp", "expert"), None),
            P("expert", None, "dp"),
            P("expert", None, "dp"),
            P("expert"),
        ),
        out_specs=(P(("dp", "expert"), None), P("expert", None, "dp"), P("expert", None, "dp")),
        check_vma=False,
    )
```

```python
import functools

import jax
import jax.numpy as jnp
from jax import lax
from jax.experimental import pallas as pl
from jax.experimental.pallas import tpu as pltpu
from jax.sharding import PartitionSpec as P

F32 = jnp.float32
BF16 = jnp.bfloat16
LOW = 8
CUTS = (8, 12, 9)
EXTRA = 16


def params(mib=48):
    return pltpu.CompilerParams(vmem_limit_bytes=mib * 2**20)


def cost(flops, values):
    return pl.CostEstimate(flops=flops, bytes_accessed=2 * values, transcendentals=0)


def xor_permute(value, axis, mask):
    pairs = [(source, source ^ mask) for source in range(lax.axis_size(axis))]
    return lax.ppermute(value, axis, pairs)


def rank_rows(first, second, experts):
    tokens = first.shape[1]
    expert = lax.broadcasted_iota(jnp.int32, (experts, tokens), 0).astype(F32)
    is_first, is_second = expert == first, expert == second
    named = jnp.where(is_first | is_second, 1.0, 0.0).astype(BF16)
    source = lax.broadcasted_iota(jnp.int32, (tokens, tokens), 0)
    target = lax.broadcasted_iota(jnp.int32, (tokens, tokens), 1)
    before = jnp.where(source < target, 1.0, 0.0).astype(BF16)
    rank = jnp.dot(named, before, preferred_element_type=F32)
    return expert, is_first, is_second, rank


def slot_rows(expert, is_first, is_second, rank, stride, base):
    place = expert * float(stride) + (rank + float(base))
    return (
        jnp.sum(jnp.where(is_first, place, 0.0), axis=0, keepdims=True),
        jnp.sum(jnp.where(is_second, place, 0.0), axis=0, keepdims=True),
    )


def one_hot(slot_first, slot_second, rows):
    row = lax.broadcasted_iota(jnp.int32, (rows, slot_first.shape[1]), 0).astype(F32)
    return jnp.where((row == slot_first) | (row == slot_second), 1.0, 0.0).astype(BF16)


def own_kernel(experts, slots, routing_ref, high_ref, rows_ref, hot_ref):
    @pl.when(pl.program_id(0) == 0)
    def _():
        info = routing_ref[...].astype(F32)
        ranks = rank_rows(info[0:1], info[1:2], experts)
        first, second = slot_rows(*ranks, slots, 0)
        hot_ref[...] = one_hot(first, second, experts * slots)

    picked = jnp.dot(hot_ref[...], high_ref[...], preferred_element_type=F32)
    rows_ref[...] = picked.reshape(rows_ref.shape).astype(BF16)


def own_rows(routing, high, experts, slots):
    tok_dev, width = high.shape
    tile = min(256, width)
    return pl.pallas_call(
        functools.partial(own_kernel, experts, slots),
        grid=(width // tile,),
        in_specs=[
            pl.BlockSpec(routing.shape, lambda i: (0, 0)),
            pl.BlockSpec((tok_dev, tile), lambda i: (0, i)),
        ],
        out_specs=pl.BlockSpec((experts, slots, tile), lambda i: (0, 0, i)),
        out_shape=jax.ShapeDtypeStruct((experts, slots, width), BF16),
        scratch_shapes=[pltpu.VMEM((experts * slots, tok_dev), BF16)],
        compiler_params=params(),
        cost_estimate=cost(2 * experts * slots * tok_dev * width, 4 * tok_dev * width),
        name="own_rows",
    )(routing, high)


def low_kernel(n, experts, slots, *refs):
    blocks = refs[:n]
    rows_ref, slots_ref, hot_ref = refs[n:]
    tok_dev = blocks[0].shape[0] - EXTRA

    @pl.when(pl.program_id(0) == 0)
    def _():
        parts = []
        for s in range(n):
            info = blocks[s][tok_dev : tok_dev + EXTRA, 0:tok_dev].astype(F32)
            ranks = rank_rows(info[0:1], info[1:2], experts)
            own = slot_rows(*ranks, slots, 0)
            full = slot_rows(*ranks, n * slots, s * slots)
            hot_ref[s] = one_hot(*own, experts * slots)
            parts.append(
                jnp.concatenate([*full, info[2:4], *own, jnp.zeros((2, tok_dev), F32)], axis=0)
            )
        slots_ref[...] = jnp.concatenate(parts, axis=1)

    for s in range(n):
        picked = jnp.dot(hot_ref[s], blocks[s][0:tok_dev, :], preferred_element_type=F32)
        rows_ref[:, s] = picked.reshape(experts, slots, picked.shape[1]).astype(BF16)


def low_rows(blocks, experts, slots):
    n = len(blocks)
    tok_dev, width = blocks[0].shape[0] - EXTRA, blocks[0].shape[1]
    tile = min(256, width)
    return pl.pallas_call(
        functools.partial(low_kernel, n, experts, slots),
        grid=(width // tile,),
        in_specs=[pl.BlockSpec((tok_dev + EXTRA, tile), lambda i: (0, i))] * n,
        out_specs=[
            pl.BlockSpec((experts, n, slots, tile), lambda i: (0, 0, 0, i)),
            pl.BlockSpec((8, n * tok_dev), lambda i: (0, 0)),
        ],
        out_shape=[
            jax.ShapeDtypeStruct((experts, n, slots, width), BF16),
            jax.ShapeDtypeStruct((8, n * tok_dev), F32),
        ],
        scratch_shapes=[pltpu.VMEM((n, experts * slots, tok_dev), BF16)],
        compiler_params=params(),
        cost_estimate=cost(40 * n * experts * slots * tok_dev * width, 100 * n * tok_dev * width),
        name="low_rows",
    )(*blocks)


def feed_kernel(n, low_ref, *refs):
    highs = refs[:n]
    inner_ref, outer_ref = refs[n : n + 2]
    low_out_ref, outs = refs[-n - 1], refs[-n:]
    depth = low_ref.shape[3]

    def flat(value):
        rows = value.shape[0] * value.shape[1]
        return value.astype(F32).reshape(rows, value.shape[2]).astype(BF16)

    def outer_dot(hidden, start, size):
        return lax.dot_general(
            hidden, outer_ref[start : start + size, :], (((1,), (1,)), ((), ())),
            preferred_element_type=F32,
        )

    for s in range(n):

        @pl.when(pl.program_id(0) == s)
        def _(s=s):
            total = jnp.dot(flat(low_ref[:, 0]), inner_ref[0:depth, :], preferred_element_type=F32)
            total += jnp.dot(flat(highs[s][...]), inner_ref[depth:, :], preferred_element_type=F32)
            hidden = jnp.maximum(total, 0.0).astype(BF16)
            experts, slots, height = outs[s].shape
            out = outer_dot(hidden, depth, height)
            outs[s][...] = out.reshape(experts, slots, height).astype(BF16)
            out = outer_dot(hidden, 0, depth)
            low_out_ref[:, 0] = out.reshape(experts, slots, depth).astype(BF16)


def feed(low, base, highs, inner, outer, *earlier):
    experts, blocks, slots, depth = low.shape
    n = len(highs)
    height = highs[0].shape[2]
    units = inner.shape[1]
    rows = n * experts * slots
    whole = pl.BlockSpec((experts, slots, height), lambda i: (0, 0, 0))
    return pl.pallas_call(
        functools.partial(feed_kernel, n),
        grid=(n,),
        in_specs=[pl.BlockSpec((experts, 1, slots, depth), lambda i: (0, base + i, 0, 0))]
        + [whole] * n
        + [pl.BlockSpec((depth + height, units), lambda i: (0, 0))] * 2
        + [pl.BlockSpec(memory_space=pl.ANY)] * len(earlier),
        out_specs=[pl.BlockSpec((experts, 1, slots, depth), lambda i: (0, base + i, 0, 0))]
        + [whole] * n,
        input_output_aliases={n + 3: 0} if earlier else {},
        out_shape=[jax.ShapeDtypeStruct((experts, blocks, slots, depth), BF16)]
        + [jax.ShapeDtypeStruct((experts, slots, height), BF16)] * n,
        compiler_params=params(),
        cost_estimate=cost(4 * rows * units * (depth + height), 2 * (rows + units) * (depth + height)),
        name="feed",
    )(low, *highs, inner, outer, *earlier)


def combine_kernel(n, first_col, cols_ref, back_ref, *refs):
    outs, gate_ref = refs[:n], refs[n]
    tok_dev = outs[0].shape[0]

    @pl.when(pl.program_id(0) == 0)
    def _():
        cols = cols_ref[...]
        slot = lax.broadcasted_iota(jnp.int32, gate_ref.shape, 1).astype(F32)
        gate = jnp.where(slot == cols[:, first_col : first_col + 1], cols[:, 2:3], 0.0)
        gate = jnp.where(slot == cols[:, first_col + 1 : first_col + 2], cols[:, 3:4], gate)
        gate_ref[...] = (gate * (1.0 / 256.0)).astype(BF16)

    total = jnp.dot(gate_ref[...], back_ref[...], preferred_element_type=F32).astype(BF16)
    for block in range(n):
        outs[block][...] = total[block * tok_dev : (block + 1) * tok_dev, :]


def combine(cols, back, n, tok_dev, first_col):
    rows, width = back.shape
    tokens = n * tok_dev
    tile = min(256, width)
    return pl.pallas_call(
        functools.partial(combine_kernel, n, first_col),
        grid=(width // tile,),
        in_specs=[
            pl.BlockSpec((tokens, 8), lambda i: (0, 0)),
            pl.BlockSpec((rows, tile), lambda i: (0, i)),
        ],
        out_specs=[pl.BlockSpec((tok_dev, tile), lambda i: (0, i))] * n,
        out_shape=[jax.ShapeDtypeStruct((tok_dev, width), BF16)] * n,
        scratch_shapes=[pltpu.VMEM((tokens, rows), BF16)],
        compiler_params=params(),
        cost_estimate=cost(2 * rows * tokens * width, (rows + tokens) * width),
        name="combine",
    )(cols, back)


def to_experts(rows):
    return lax.all_to_all(rows, "expert", split_axis=0, concat_axis=0, tiled=True)


def add_up(parts):
    total = parts[0].astype(F32)
    for part in parts[1:]:
        total = total + part.astype(F32)
    return total.astype(BF16)


def fetch(parts, base):
    return [xor_permute(part, "dp", base + s) for s, part in enumerate(parts)]


def spread(value, n):
    values = [value]
    for s in range(1, n):
        values.append(xor_permute(values[s & (s - 1)], "dp", s & -s))
    return values


def fold(parts):
    parts = list(parts)
    for s in range(len(parts) - 1, 0, -1):
        rest = s & (s - 1)
        parts[rest] = add_up([parts[rest], xor_permute(parts[s], "dp", s & -s)])
    return parts[0]


def share_of(weight, start, size):
    return lax.slice_in_dim(weight, start, start + size, axis=1)


def with_trade(flag, weight, start, size, work, *operands):
    mask = lax.axis_size("expert") // 2

    def trading(w, *values):
        return xor_permute(share_of(w, start, size), "expert", mask), work(*values)

    def staying(w, *values):
        return share_of(w, start, size), work(*values)

    return lax.cond(flag, trading, staying, weight, *operands)


def with_last_trade(flag, weight, start, placed, work, *operands):
    mask = lax.axis_size("expert") // 2
    size = weight.shape[1] - start

    def base(w, placed):
        both = jnp.concatenate([placed, share_of(w, start, size)], axis=1)
        return lax.optimization_barrier(both)

    def trading(w, placed, *values):
        moved = xor_permute(share_of(w, start, size), "expert", mask)
        result = work(*values)
        return lax.dynamic_update_slice_in_dim(base(w, placed), moved, start, axis=1), result

    def staying(w, placed, *values):
        return base(w, placed), work(*values)

    return lax.cond(flag, trading, staying, weight, placed, *operands)


def after(value, *others):
    return lax.optimization_barrier((value, *others))[0]


def local(tokens, expert_ids, gate_levels, inner_weight, outer_weight, pair_flags):
    n_dp = lax.axis_size("dp")
    n_expert = lax.axis_size("expert")
    tok_dev, width = tokens.shape
    depth = width * LOW // 16
    experts = n_expert * inner_weight.shape[0]
    capacity = max(2, 9 * tok_dev // (4 * experts))
    slots = -(-capacity // 8) * 8
    group = n_dp // 2
    flag = pair_flags[0] == 1
    rows_in = inner_weight.shape[1]
    cut_a, cut_b = rows_in * CUTS[0] // 16, rows_in * CUTS[1] // 16
    share = rows_in * CUTS[2] // 16
    inner, outer = inner_weight[0], outer_weight[0]

    routing = jnp.concatenate([expert_ids.T, gate_levels.T], axis=0).astype(BF16)
    routing = jnp.pad(routing, ((0, EXTRA - 4), (0, 0)))
    low = jnp.concatenate(
        [tokens[:, :depth], jnp.pad(routing, ((0, 0), (0, depth - tok_dev)))], axis=0
    )
    own = own_rows(routing, tokens[:, depth:], experts, slots)
    high = to_experts(own)

    lows = [low, *fetch([low] * (n_dp - 1), 1)]
    inner_a, _ = with_trade(after(flag, own), inner_weight, 0, cut_a, lambda: ())
    high, inner_a = lax.optimization_barrier((high, inner_a))
    *lows, inner_a = lax.optimization_barrier((*lows, inner_a))
    rows, info = low_rows(lows, experts, slots)
    moved = to_experts(rows.reshape(experts, n_dp * slots, depth)).reshape(rows.shape)
    highs = spread(high, n_dp)

    def first_half(moved, inner, outer, *highs):
        return tuple(feed(moved, 0, highs, inner, outer))

    inner_b, (low_a, *high_a) = with_trade(
        flag, inner_weight, cut_a, cut_b - cut_a, first_half, moved, inner, outer, *highs[:group]
    )
    *later, low_a = lax.optimization_barrier((*highs[group:], low_a))

    def second_half(moved, inner, outer, low_a, *highs):
        done, sent = highs[: n_dp - group], highs[n_dp - group :]
        return tuple(feed(moved, group, done, inner, outer, low_a)), fold(sent)

    inner_c, ((out_low, *high_b), folded) = with_trade(
        flag, inner_weight, cut_b, rows_in - cut_b, second_half,
        moved, inner, outer, low_a, *later, *high_a,
    )
    back = to_experts(out_low.reshape(experts, n_dp * slots, depth))

    def third(*high_b):
        return xor_permute(fold(high_b), "dp", group)

    outer_a, got = with_trade(
        after(flag, out_low), outer_weight, 0, share, third, *high_b
    )
    summed = add_up([folded, got])
    cols = info.T
    parts = combine(cols, back.reshape(experts * n_dp * slots, depth), n_dp, tok_dev, 0)
    back_own = to_experts(after(summed, parts[0]))
    def last(inner_a, inner_b, inner_c, *parts):
        placed_inner = jnp.concatenate([inner_a, inner_b, inner_c], axis=1)
        return placed_inner, add_up([parts[0], *fetch(parts[1:], 1)])

    placed_outer, (placed_inner, mixed_low) = with_last_trade(
        after(flag, summed, parts[0]), outer_weight, share, outer_a, last,
        inner_a, inner_b, inner_c, *parts,
    )
    [mixed_high] = combine(
        cols[0:tok_dev], back_own.reshape(experts * slots, width - depth), 1, tok_dev, 4
    )
    mixture = jnp.concatenate([mixed_low, mixed_high], axis=1)
    return mixture, placed_inner, placed_outer


def solution(mesh):
    return jax.shard_map(
        local,
        mesh=mesh,
        in_specs=(
            P(("dp", "expert"), None),
            P(("dp", "expert"), None),
            P(("dp", "expert"), None),
            P("expert", None, "dp"),
            P("expert", None, "dp"),
            P("expert"),
        ),
        out_specs=(P(("dp", "expert"), None), P("expert", None, "dp"), P("expert", None, "dp")),
        check_vma=False,
    )
```
